256 devices in a mesh: sta: 32 (over z, y_lo, core), freq: 8 (over x, y_hi).
Axes of the slice: x: 4, y: 4 (y_hi: 2, y_lo: 2; y = y_hi * 2 + y_lo), z: 8, core: 2. Of those that a mesh axis runs over, the one named last changes fastest.
Arguments:
- spectra: bfloat16 [2, 768, 4096], P(None, 'sta', 'freq'), may hold values from -6 to 6
- pair_mask: int32 [32, 32], replicated, may hold values from 0 to 1, as said below
Outputs:
- correlograms: bfloat16 [32, 17, 24, 24, 512], P('sta', None, 'freq')
The draws below stay inside these ranges and needn't reach their ends.
Inputs may be any that keep to these rules, and one draw needn't show every extreme that they name: pair_mask is symmetric and its diagonal is 1.
All inputs are finite; a program needn't handle non-finite values.
Results may differ from the reference program's by a relative error of at most 0.0055.
Values may be sent and summed in bfloat16 or wider, within the bound.
A program may use at most 64 MiB of HBM per device.

```python
import math
import jax
import jax.numpy as jnp
from jax import lax

STA_DEV = 24
FREQS = 4096
LAGS = 512
BLOCKS = 32
STATIONS = 768
OFFSETS = 17


def draw_pair_mask(key, part):
    key = jax.random.fold_in(key, 11)
    spots = jax.random.randint(key, (BLOCKS, 2), 0, 6)
    spots = spots.at[0].set(0).at[1].set(5)
    apart = spots[:, None, :] - spots[None, :, :]
    reach = jnp.sum(apart * apart, axis=-1)
    return (reach <= 5).astype(jnp.int32)


def levels(rng, dims, cuts, low, top_value):
    def one(dim, shards_of):
        draws = jax.random.uniform(jax.random.fold_in(jax.random.fold_in(rng, 6), dim), (shards_of,), jnp.float32, low / len(cuts), top_value / len(cuts))
        return jnp.repeat(jnp.exp(draws), dims[dim] // shards_of).reshape((-1,) + (1,) * (len(dims) - dim - 1))

    loudness = one(*cuts[0])
    for cut in cuts[1:]:
        loudness = loudness * one(*cut)
    return loudness


def bell_draw(key, dims, width, limit, split=(), held_as=jnp.bfloat16):
    gain = levels(key, dims, split, -0.22, 0.18) if split else 1.0
    values = jax.random.normal(key, dims, jnp.float32) * width * gain
    return jnp.minimum(jnp.maximum(values, -limit), limit).astype(held_as)


def setup_inputs(seed: int = 0) -> dict:
    keys = jax.random.split(jax.random.key(seed), 3)
    return {
        "spectra": bell_draw(keys[0], (2, STATIONS, FREQS), 1.0, 6.0, ((1, 32), (2, 8))),
        "pair_mask": draw_pair_mask(jax.random.fold_in(keys[2], 71), 0),
    }


def lag_table(first, count):
    bins = first + jnp.arange(count, dtype=jnp.int32)
    shifts = jnp.arange(LAGS, dtype=jnp.int32) - LAGS // 2
    phase = bins[:, None] * shifts[None, :] % (2 * FREQS)
    angle = math.pi * phase.astype(jnp.float32) / FREQS
    factor = 1.0 / math.sqrt(FREQS)
    return jnp.concatenate([jnp.cos(angle) * factor, -jnp.sin(angle) * factor], axis=0).astype(jnp.bfloat16)

def cross_spectra(mine, other):
    real_a = mine[0].astype(jnp.float32)[:, None, :]
    imag_a = mine[1].astype(jnp.float32)[:, None, :]
    real_b = other[0].astype(jnp.float32)[None, :, :]
    imag_b = other[1].astype(jnp.float32)[None, :, :]
    real_part = real_a * real_b + imag_a * imag_b
    imag_part = imag_a * real_b - real_a * imag_b
    return jnp.concatenate([real_part, imag_part], axis=2).astype(jnp.bfloat16)

def reference(spectra, pair_mask):
    blocks = spectra.reshape(2, BLOCKS, STA_DEV, FREQS)
    table = lag_table(0, FREQS)
    distinct = 1.0 - jnp.eye(STA_DEV, dtype=jnp.float32)

    def single(index):
        block = (index // OFFSETS).astype(jnp.int32)
        offset = (index % OFFSETS).astype(jnp.int32)
        other_block = ((block + offset) % BLOCKS).astype(jnp.int32)
        mine = lax.dynamic_index_in_dim(blocks, block, axis=1, keepdims=False)
        other = lax.dynamic_index_in_dim(blocks, other_block, axis=1, keepdims=False)
        flag = pair_mask[block, other_block]

        def compute(operands):
            product = cross_spectra(operands[0], operands[1]).reshape(STA_DEV * STA_DEV, 2 * FREQS)
            return jnp.dot(product, table, preferred_element_type=jnp.float32).reshape(STA_DEV, STA_DEV, LAGS)

        def nothing(operands):
            return jnp.zeros((STA_DEV, STA_DEV, LAGS), jnp.float32)
        value = lax.cond(flag > 0, compute, nothing, (mine, other))
        keep = jnp.where(offset == 0, distinct, jnp.ones_like(distinct))
        return (value * keep[:, :, None]).astype(jnp.bfloat16)
    result = lax.map(single, jnp.arange(BLOCKS * OFFSETS, dtype=jnp.int32))
    return result.reshape(BLOCKS, OFFSETS, STA_DEV, STA_DEV, LAGS)
```

```python
import functools
import math

import jax
import jax.numpy as jnp
import ml_dtypes
import numpy as np
from jax import lax
from jax.experimental import pallas as pl
from jax.experimental.pallas import tpu as pltpu
from jax.sharding import PartitionSpec as P

FREQS = 4096
LAGS = 512
HALF = LAGS // 2
STA = 24
BAND = 512
BANDS = 8
OWN = 3
UNITS = 4
PER_UNIT = 4
PAIRS = PER_UNIT * OWN
ROWS = PAIRS * STA
MAIN = 32
LEFT = 4
MESH = pl.DeviceIdType.MESH
F32 = jnp.float32
BF16 = jnp.bfloat16


def half_tables():
    bins = np.arange(FREQS, dtype=np.float64)[:, None]
    lags = np.arange(HALF, dtype=np.float64)[None, :] + 0.5
    angle = math.pi * bins * lags / FREQS
    both = np.concatenate([np.cos(angle), np.sin(angle)], axis=1) / math.sqrt(FREQS)
    return both.astype(np.float32).astype(ml_dtypes.bfloat16).reshape(BANDS, BAND, LAGS)


def phases():
    angle = math.pi * np.arange(FREQS, dtype=np.float64) / (2 * FREQS)
    both = np.stack([np.cos(angle), np.sin(angle)])
    return both.reshape(2 * BANDS, 1, BAND).astype(np.float32)


def piece_select():
    select = np.zeros((4, BANDS * 16, STA), np.float32)
    for dest in range(BANDS):
        for jj in range(OWN):
            for part in range(2):
                for half in range(2):
                    row = dest * 16 + (jj * 2 + part) * 2 + half
                    select[part * 2 + half, row, OWN * dest + jj] = 1
    return select.astype(ml_dtypes.bfloat16)


def send_select():
    select = np.zeros((BANDS * (MAIN + LEFT), ROWS), np.float32)
    for dest in range(BANDS):
        for kk in range(PER_UNIT):
            for il in range(OWN):
                for jj in range(OWN):
                    r = kk * 9 + il * OWN + jj
                    row = dest * MAIN + r if r < MAIN else BANDS * MAIN + dest * LEFT + r - MAIN
                    select[row, (kk * OWN + jj) * STA + OWN * dest + il] = 1
    return select.astype(ml_dtypes.bfloat16)


def left_select():
    select = np.zeros((128, 128), np.float32)
    for unit in range(UNITS):
        for dest in range(BANDS):
            for r in range(LEFT):
                select[dest * 16 + unit * LEFT + r, unit * 32 + dest * LEFT + r] = 1
    return select.astype(ml_dtypes.bfloat16)


def final_select():
    first = np.zeros((216, 256), np.float32)
    last = np.zeros((72, 256), np.float32)
    left = np.zeros((UNITS, 72, 128), np.float32)
    for source in range(BANDS):
        for il in range(OWN):
            for jj in range(OWN):
                row = il * STA + OWN * source + jj
                nine = il * OWN + jj
                for kk in range(3):
                    first[kk * 72 + row, source * MAIN + kk * 9 + nine] = 1
                if nine < 5:
                    last[row, source * MAIN + 27 + nine] = 1
                else:
                    for unit in range(UNITS):
                        left[unit, row, source * 16 + unit * LEFT + nine - 5] = 1
    cast = ml_dtypes.bfloat16
    return first.astype(cast), last.astype(cast), left.astype(cast)


def flip():
    return np.eye(HALF, dtype=np.float32)[::-1].astype(ml_dtypes.bfloat16)


def dot(a, b):
    return jnp.dot(a, b, preferred_element_type=F32)


def kernel(
    x_ref, mask_ref, phase_ref, piece_ref, send_ref, lefts_ref, first_ref, last_ref, left_ref, flip_ref, table_hbm,
    out_ref,
    table, pieces, b_land, a_land, a_spec, b_spec, lre0, lim0, lre1, lim1, acc, prod, s_main, s_lefts, s_left, m_main, m_left,
    table_sem, b_send, b_recv, a_send, a_recv, ring_send, ring_recv, sib_send, sib_recv, o_send, o_recv, l_send, l_recv,
):
    sta, freq = lax.axis_index("sta"), lax.axis_index("freq")
    z, quad = sta // 4, sta % 4
    ylo, core = quad // 2, quad % 2
    xx, yhi = freq // 2, freq % 2

    fetch = pltpu.make_async_copy(table_hbm, table, table_sem)
    fetch.start()

    def peer(dx, dh, dl):
        return (
            z * 4 + (ylo + dl) % 2 * 2 + core,
            (xx + dx) % 4 * 2 + (yhi + dh) % 2,
        )

    plane = [(dx, dh, dl) for dl in range(2) for dh in range(2) for dx in range(4)]
    others = plane[1:]
    group = [d for d in others if d[2] == 0]
    below = ((sta + 28) % 32, freq)
    above = ((sta + 4) % 32, freq)
    sibling = (z * 4 + ylo * 2 + (1 - core), freq)

    barrier = pltpu.get_barrier_semaphore()
    for device in [peer(*d) for d in others] + [sibling, above]:
        pl.semaphore_signal(barrier, inc=1, device_id=device, device_id_type=MESH)

    total = None
    for part in range(2):
        for half in range(2):
            term = dot(piece_ref[part * 2 + half], x_ref[part, :, half * 256 : half * 256 + 256])
            total = term if total is None else total + term
    pieces[...] = total.astype(BF16).reshape(BANDS, 16, 256)

    pl.semaphore_wait(barrier, len(others) + 2)

    def remote(src, dst, send, recv, device):
        return pltpu.make_async_remote_copy(
            src_ref=src, dst_ref=dst, send_sem=send, recv_sem=recv, device_id=device, device_id_type=MESH
        )

    b_copies = []
    for n, d in enumerate(others):
        device = peer(*d)
        b_copies.append(
            remote(pieces.at[device[1]], b_land.at[0, core, ylo, freq], b_send.at[n], b_recv.at[n], device)
        )
    a_copies = []
    for n, d in enumerate(group):
        a_copies.append(remote(x_ref, a_land.at[freq], a_send.at[n], a_recv.at[n], peer(*d)))
    for copy in b_copies + a_copies:
        copy.start()
    b_land[0, core, ylo, freq] = pieces[freq]
    a_land[freq] = x_ref[...]

    def ring(s, part):
        return remote(
            b_land.at[s, core, part], b_land.at[s + 1, core, part], ring_send.at[s, part], ring_recv.at[s, part], below
        )

    def across(s, part):
        return remote(
            b_land.at[s, core, part], b_land.at[s, core, part], sib_send.at[s, part], sib_recv.at[s, part], sibling
        )

    def forward(s):
        for part in range(2):
            if s > 0:
                ring(s - 1, part).wait_recv()
            if s < UNITS:
                ring(s, part).start()
            across(s, part).start()

    for copy in b_copies:
        copy.wait_recv()
    forward(0)

    for copy in a_copies:
        copy.wait_recv()

    def rotate(h, carry):
        cos, sin = phase_ref[h], phase_ref[BANDS + h]
        re = a_land[h, 0].astype(F32)
        im = a_land[h, 1].astype(F32)
        a_spec[h, 0] = re * cos + im * sin
        a_spec[h, 1] = im * cos - re * sin
        return carry

    lax.fori_loop(0, BANDS, rotate, 0)
    fetch.wait()

    def project(buffers, h, rows):
        lre, lim = buffers
        acc[:rows, :HALF] += dot(lre[:rows], table[h, :, :HALF])
        acc[:rows, HALF:] += dot(lim[:rows], table[h, :, HALF:])

    def products(cross, rows):
        acc[:rows] = jnp.zeros((rows, LAGS), F32)
        even, odd = (lre0, lim0), (lre1, lim1)
        cross(0, even)

        def step(i, carry):
            cross(2 * i + 1, odd)
            project(even, 2 * i, rows)
            cross(2 * i + 2, even)
            project(odd, 2 * i + 1, rows)
            return carry

        lax.fori_loop(0, 3, step, 0)
        cross(7, odd)
        project(even, 6, rows)
        project(odd, 7, rows)
        cos, sin = acc[:rows, :HALF], acc[:rows, HALF:]
        return (cos + sin).astype(BF16), (cos - sin).astype(BF16)

    def cross_unit(h, buffers):
        for half in range(2):
            lanes = slice(half * 256, half * 256 + 256)
            ar, ai = a_spec[h, 0, :, lanes], a_spec[h, 1, :, lanes]
            for two in range(PAIRS // 2):
                re, im = [], []
                for g in (2 * two, 2 * two + 1):
                    kk, jj = g // OWN, g % OWN
                    row = jj * 4 + half
                    br = b_spec[h, kk, row : row + 1, :]
                    bi = b_spec[h, kk, row + 2 : row + 3, :]
                    re.append(ar * br + ai * bi)
                    im.append(ai * br - ar * bi)
                buffers[0][two * 48 : two * 48 + 48, lanes] = jnp.concatenate(re, axis=0).astype(BF16)
                buffers[1][two * 48 : two * 48 + 48, lanes] = jnp.concatenate(im, axis=0).astype(BF16)

    def cross_own(h, buffers):
        for half in range(2):
            lanes = slice(half * 256, half * 256 + 256)
            br = a_land[h, 0, :, lanes].astype(F32)
            bi = a_land[h, 1, :, lanes].astype(F32)
            re, im = [], []
            for il in (0, 1, 2, 2):
                ar = a_spec[h, 0, pl.ds(OWN * freq + il, 1), lanes]
                ai = a_spec[h, 1, pl.ds(OWN * freq + il, 1), lanes]
                re.append(ar * br + ai * bi)
                im.append(ai * br - ar * bi)
            buffers[0][:96, lanes] = jnp.concatenate(re, axis=0).astype(BF16)
            buffers[1][:96, lanes] = jnp.concatenate(im, axis=0).astype(BF16)

    def out_copies(unit):
        copies = []
        for n, d in enumerate(group):
            device = peer(*d)
            copies.append(
                remote(s_main.at[unit, device[1]], m_main.at[unit, freq], o_send.at[unit, n], o_recv.at[unit, n], device)
            )
        return copies

    def left_copies():
        copies = []
        for n, d in enumerate(group):
            device = peer(*d)
            copies.append(remote(s_left.at[device[1]], m_left.at[freq], l_send.at[n], l_recv.at[n], device))
        return copies

    def write(offset, value, keep=None):
        on = mask_ref[sta, (sta + offset) % 32] > 0
        value = jnp.where(on, value, 0.0)
        if keep is not None:
            value = jnp.where(keep, value, 0.0)
        out_ref[offset] = value.reshape(OWN, STA, LAGS).astype(BF16)

    def finish(unit):
        for copy in out_copies(unit):
            copy.wait_recv()
        rows = dot(first_ref[...], m_main[unit].reshape(256, LAGS))
        low = dot(rows[:, :HALF].astype(BF16), flip_ref[...])
        rows = jnp.concatenate([low, rows[:, HALF:]], axis=1)
        for kk in range(3):
            write(unit * PER_UNIT + 1 + kk, rows[kk * 72 : kk * 72 + 72])

    for unit in range(UNITS):
        forward(unit + 1)
        for s in ([0, 1] if unit == 0 else [unit + 1]):
            for part in range(2):
                across(s, part).wait_recv()
        for kk in range(PER_UNIT):
            slot = quad + unit * PER_UNIT + 1 + kk
            spot = slot % 4
            b_spec[:, kk] = b_land[slot // 4, spot % 2, spot // 2].astype(F32)
        low, high = products(cross_unit, ROWS)
        prod[:, :HALF] = low
        prod[:, HALF:] = high
        rows = dot(send_ref[...], prod[...])
        s_main[unit] = rows[:256].astype(BF16).reshape(BANDS, MAIN, LAGS)
        s_lefts[unit] = rows[256:].astype(BF16)
        for copy in out_copies(unit):
            copy.start()
        m_main[unit, freq] = s_main[unit, freq]
        if unit > 0:
            finish(unit - 1)

    s_left[...] = dot(lefts_ref[...], s_lefts[...].reshape(128, LAGS)).astype(BF16).reshape(BANDS, 16, LAGS)
    for copy in left_copies():
        copy.start()
    m_left[freq] = s_left[freq]

    low, high = products(cross_own, 96)
    low = dot(low, flip_ref[...])
    value = jnp.concatenate([low, high.astype(F32)], axis=1)[:72]
    row = lax.broadcasted_iota(jnp.int32, (72, LAGS), 0)
    mine = row // STA + OWN * freq
    write(0, value, row % STA != mine)

    finish(UNITS - 1)
    for copy in left_copies():
        copy.wait_recv()
    for unit in range(UNITS):
        rows = dot(last_ref[...], m_main[unit].reshape(256, LAGS)) + dot(left_ref[unit], m_left[...].reshape(128, LAGS))
        low = dot(rows[:, :HALF].astype(BF16), flip_ref[...])
        write(unit * PER_UNIT + 4, jnp.concatenate([low, rows[:, HALF:]], axis=1))

    for copy in b_copies + a_copies + left_copies():
        copy.wait_send()
    for unit in range(UNITS):
        for copy in out_copies(unit):
            copy.wait_send()
        for part in range(2):
            ring(unit, part).wait_send()
    for s in range(UNITS + 1):
        for part in range(2):
            across(s, part).wait_send()


def local(spectra, pair_mask):
    first, last, left = final_select()
    small = [phases(), piece_select(), send_select(), left_select(), first, last, left, flip()]
    vmem = pl.BlockSpec(memory_space=pltpu.VMEM)
    dma = pltpu.SemaphoreType.DMA
    out = pl.pallas_call(
        kernel,
        out_shape=jax.ShapeDtypeStruct((17, OWN, STA, LAGS), BF16),
        in_specs=[vmem, pl.BlockSpec(memory_space=pltpu.SMEM)] + [vmem] * len(small) + [pl.BlockSpec(memory_space=pl.ANY)],
        out_specs=vmem,
        scratch_shapes=[
            pltpu.VMEM((BANDS, BAND, LAGS), BF16),
            pltpu.VMEM((BANDS, 16, 256), BF16),
            pltpu.VMEM((UNITS + 1, 2, 2, BANDS, 16, 256), BF16),
            pltpu.VMEM((BANDS, 2, STA, BAND), BF16),
            pltpu.VMEM((BANDS, 2, STA, BAND), F32),
            pltpu.VMEM((BANDS, PER_UNIT, 16, 256), F32),
            pltpu.VMEM((ROWS, BAND), BF16),
            pltpu.VMEM((ROWS, BAND), BF16),
            pltpu.VMEM((ROWS, BAND), BF16),
            pltpu.VMEM((ROWS, BAND), BF16),
            pltpu.VMEM((ROWS, LAGS), F32),
            pltpu.VMEM((ROWS, LAGS), BF16),
            pltpu.VMEM((UNITS, BANDS, MAIN, LAGS), BF16),
            pltpu.VMEM((UNITS, BANDS * LEFT, LAGS), BF16),
            pltpu.VMEM((BANDS, 16, LAGS), BF16),
            pltpu.VMEM((UNITS, BANDS, MAIN, LAGS), BF16),
            pltpu.VMEM((BANDS, 16, LAGS), BF16),
            dma,
            dma((15,)),
            dma((15,)),
            dma((7,)),
            dma((7,)),
            dma((UNITS, 2)),
            dma((UNITS, 2)),
            dma((UNITS + 1, 2)),
            dma((UNITS + 1, 2)),
            dma((UNITS, 7)),
            dma((UNITS, 7)),
            dma((7,)),
            dma((7,)),
        ],
        compiler_params=pltpu.CompilerParams(
            collective_id=0, has_side_effects=True, vmem_limit_bytes=48 * 1024 * 1024
        ),
        cost_estimate=pl.CostEstimate(flops=10_000_000_000, bytes_accessed=8_000_000, transcendentals=0),
        name="correlate",
    )(spectra, pair_mask, *[jnp.asarray(value) for value in small], jnp.asarray(half_tables()))
    return out[None]


def solution(mesh):
    return jax.shard_map(
        local,
        mesh=mesh,
        in_specs=(P(None, "sta", "freq"), P()),
        out_specs=P("sta", None, "freq", None, None),
        check_vma=False,
    )
```

```python
import functools
import math

import jax
import jax.numpy as jnp
import ml_dtypes
import numpy as np
from jax import lax
from jax.experimental import pallas as pl
from jax.experimental.pallas import tpu as pltpu
from jax.sharding import PartitionSpec as P

FREQS = 4096
LAGS = 512
HALF = LAGS // 2
STA = 24
BAND = 512
BANDS = 8
OWN = 3
UNITS = 4
PER_UNIT = 4
PAIRS = PER_UNIT * OWN
ROWS = PAIRS * STA
MAIN = 32
LEFT = 4
WIDE = 2 * LAGS + 128
INPUTS = 6
PARTS = 4
MESH = pl.DeviceIdType.MESH
F32 = jnp.float32
BF16 = jnp.bfloat16


def half_tables():
    bins = np.arange(FREQS, dtype=np.float64)[:, None]
    lags = np.arange(HALF, dtype=np.float64)[None, :] + 0.5
    angle = math.pi * bins * lags / FREQS
    both = np.concatenate([np.cos(angle), np.sin(angle)], axis=1) / math.sqrt(FREQS)
    return both.astype(np.float32).astype(ml_dtypes.bfloat16).reshape(BANDS, BAND, LAGS)


def padded(value):
    return np.pad(value, [(0, 0)] * (value.ndim - 2) + [(0, 8), (0, 0)])


def phases():
    angle = math.pi * np.arange(FREQS, dtype=np.float64) / (2 * FREQS)
    both = np.stack([np.cos(angle), np.sin(angle)])
    return both.reshape(2 * BANDS, 1, BAND).astype(np.float32)


def piece_select():
    select = np.zeros((4, BANDS * 16, STA), np.float32)
    for dest in range(BANDS):
        for jj in range(OWN):
            for part in range(2):
                for half in range(2):
                    row = dest * 16 + (jj * 2 + part) * 2 + half
                    select[part * 2 + half, row, OWN * dest + jj] = 1
    return select.astype(ml_dtypes.bfloat16)


def send_select():
    select = np.zeros((BANDS * (MAIN + 16), ROWS), np.float32)
    for dest in range(BANDS):
        for kk in range(PER_UNIT):
            for il in range(OWN):
                for jj in range(OWN):
                    r = kk * 9 + il * OWN + jj
                    column = (kk * OWN + jj) * STA + OWN * dest + il
                    if r < MAIN:
                        select[dest * MAIN + r, column] = 1
                    else:
                        for tile in range(4):
                            select[BANDS * MAIN + dest * 16 + tile * LEFT + r - MAIN, column] = 1
    return select.astype(ml_dtypes.bfloat16)


def final_select():
    main = np.zeros((ROWS, BANDS * MAIN), np.float32)
    left = np.zeros((4 * 72, BANDS * 16), np.float32)
    for source in range(BANDS):
        for kk in range(PER_UNIT):
            for il in range(OWN):
                for jj in range(OWN):
                    r = kk * 9 + il * OWN + jj
                    row = il * STA + OWN * source + jj
                    if r < MAIN:
                        main[kk * 72 + row, r // 16 * 128 + source * 16 + r % 16] = 1
                    else:
                        for tile in range(4):
                            left[tile * 72 + row, source * 16 + tile * LEFT + r - MAIN] = 1
    return main.astype(ml_dtypes.bfloat16), left.astype(ml_dtypes.bfloat16)


def flip():
    return np.eye(HALF, dtype=np.float32)[::-1].astype(ml_dtypes.bfloat16)


def dot(a, b):
    return jnp.dot(a, b, preferred_element_type=F32)


def kernel(
    *refs,
):
    inputs, m_out, own_out, refs = refs[:INPUTS], refs[INPUTS], refs[INPUTS + 1], refs[INPUTS + 2 :]
    held, refs = refs[:INPUTS], refs[INPUTS:]
    x_ref, piece_ref, phase_ref, table, send_ref, flip_ref = held
    (
    pieces, b_land, a_land, a_spec, b_spec, lre0, lim0, lre1, lim1, acc, prod, s_main, own,
    in_sem, b_send, b_recv, a_send, a_recv, ring_send, ring_recv, sib_send, sib_recv, o_send, o_recv, m_sem, own_sem,
    ) = refs
    sta, freq = lax.axis_index("sta"), lax.axis_index("freq")
    z, quad = sta // 4, sta % 4
    ylo, core = quad // 2, quad % 2
    xx, yhi = freq // 2, freq % 2

    fetches = [pltpu.make_async_copy(inputs[n], held[n], in_sem.at[n]) for n in range(INPUTS)]
    for fetch in fetches:
        fetch.start()

    def peer(dx, dh, dl, dz=0):
        return (
            (z + 8 - dz) % 8 * 4 + (ylo + dl) % 2 * 2 + core,
            (xx + dx) % 4 * 2 + (yhi + dh) % 2,
        )

    plane = [(dx, dh, dl) for dl in range(2) for dh in range(2) for dx in range(4)]
    others = plane[1:]
    group = [d for d in others if d[2] == 0]
    below = ((sta + 28) % 32, freq)
    nearby = [(*d, 0) for d in others] + [(*d, 1) for d in plane]
    sibling = (z * 4 + ylo * 2 + (1 - core), freq)

    barrier = pltpu.get_barrier_semaphore()
    for device in [peer(dx, dh, dl, -dz) for dx, dh, dl, dz in nearby] + [sibling]:
        pl.semaphore_signal(barrier, inc=1, device_id=device, device_id_type=MESH)

    fetches[0].wait()
    fetches[1].wait()
    total = None
    for part in range(2):
        for half in range(2):
            term = dot(piece_ref[part * 2 + half, :128], x_ref[part, :, half * 256 : half * 256 + 256])
            total = term if total is None else total + term
    pieces[...] = total.astype(BF16).reshape(BANDS, 16, 256)

    pl.semaphore_wait(barrier, len(nearby) + 1)

    def remote(src, dst, send, recv, device):
        return pltpu.make_async_remote_copy(
            src_ref=src, dst_ref=dst, send_sem=send, recv_sem=recv, device_id=device, device_id_type=MESH
        )

    b_copies = []
    for n, d in enumerate(nearby):
        device = peer(*d)
        b_copies.append(
            remote(pieces.at[device[1]], b_land.at[d[3], core, ylo, freq], b_send.at[n], b_recv.at[n], device)
        )
    a_copies = []
    for n, d in enumerate(group):
        a_copies.append(remote(x_ref, a_land.at[freq], a_send.at[n], a_recv.at[n], peer(*d)))
    for copy in b_copies + a_copies:
        copy.start()
    b_land[0, core, ylo, freq] = pieces[freq]
    a_land[freq] = x_ref[...]

    def ring(s, part):
        y, h = part // 2, pl.ds(part % 2 * 4, 4)
        return remote(
            b_land.at[s, core, y, h], b_land.at[s + 1, core, y, h], ring_send.at[s, part], ring_recv.at[s, part], below
        )

    def across(s, part):
        y, h = part // 2, pl.ds(part % 2 * 4, 4)
        return remote(
            b_land.at[s, core, y, h], b_land.at[s, core, y, h], sib_send.at[s, part], sib_recv.at[s, part], sibling
        )

    def forward(s):
        for part in range(PARTS):
            if s > 1:
                ring(s - 1, part).wait_recv()
            if 0 < s < UNITS:
                ring(s, part).start()
            across(s, part).start()

    for copy in b_copies:
        copy.wait_recv()
    forward(1)
    forward(0)

    for copy in a_copies:
        copy.wait_recv()

    def rotate(h, carry):
        cos, sin = phase_ref[h], phase_ref[BANDS + h]
        re = a_land[h, 0].astype(F32)
        im = a_land[h, 1].astype(F32)
        a_spec[h, 0] = re * cos + im * sin
        a_spec[h, 1] = im * cos - re * sin
        return carry

    fetches[2].wait()
    lax.fori_loop(0, BANDS, rotate, 0)
    for fetch in fetches[3:]:
        fetch.wait()

    def project(buffers, h, rows):
        lre, lim = buffers
        acc[:rows, :HALF] += dot(lre[:rows], table[h, :BAND, :HALF])
        acc[:rows, HALF:] += dot(lim[:rows], table[h, :BAND, HALF:])

    def products(cross, rows):
        acc[:rows] = jnp.zeros((rows, LAGS), F32)
        even, odd = (lre0, lim0), (lre1, lim1)
        cross(0, even)

        def step(i, carry):
            cross(2 * i + 1, odd)
            project(even, 2 * i, rows)
            cross(2 * i + 2, even)
            project(odd, 2 * i + 1, rows)
            return carry

        lax.fori_loop(0, 3, step, 0)
        cross(7, odd)
        project(even, 6, rows)
        project(odd, 7, rows)
        cos, sin = acc[:rows, :HALF], acc[:rows, HALF:]
        return (cos + sin).astype(BF16), (cos - sin).astype(BF16)

    def cross_unit(h, buffers):
        for half in range(2):
            lanes = slice(half * 256, half * 256 + 256)
            ar, ai = a_spec[h, 0, :, lanes], a_spec[h, 1, :, lanes]
            for two in range(PAIRS // 2):
                re, im = [], []
                for g in (2 * two, 2 * two + 1):
                    kk, jj = g // OWN, g % OWN
                    row = jj * 4 + half
                    br = b_spec[h, kk, row : row + 1, :]
                    bi = b_spec[h, kk, row + 2 : row + 3, :]
                    re.append(ar * br + ai * bi)
                    im.append(ai * br - ar * bi)
                buffers[0][two * 48 : two * 48 + 48, lanes] = jnp.concatenate(re, axis=0).astype(BF16)
                buffers[1][two * 48 : two * 48 + 48, lanes] = jnp.concatenate(im, axis=0).astype(BF16)

    def cross_own(h, buffers):
        for half in range(2):
            lanes = slice(half * 256, half * 256 + 256)
            br = a_land[h, 0, :, lanes].astype(F32)
            bi = a_land[h, 1, :, lanes].astype(F32)
            re, im = [], []
            for il in (0, 1, 2, 2):
                ar = a_spec[h, 0, pl.ds(OWN * freq + il, 1), lanes]
                ai = a_spec[h, 1, pl.ds(OWN * freq + il, 1), lanes]
                re.append(ar * br + ai * bi)
                im.append(ai * br - ar * bi)
            buffers[0][:96, lanes] = jnp.concatenate(re, axis=0).astype(BF16)
            buffers[1][:96, lanes] = jnp.concatenate(im, axis=0).astype(BF16)

    def out_copies(unit):
        copies = []
        for n, d in enumerate(group):
            device = peer(*d)
            copies.append(
                remote(s_main.at[unit, device[1]], m_out.at[unit, freq], o_send.at[unit, n], o_recv.at[unit, n], device)
            )
        return copies

    def kept(unit):
        return pltpu.make_async_copy(s_main.at[unit, freq], m_out.at[unit, freq], m_sem.at[unit])

    tile = lax.broadcasted_iota(jnp.int32, (BANDS * 16, 128), 0) // LEFT % 4

    for unit in range(UNITS):
        if unit + 2 <= UNITS:
            forward(unit + 2)
        for s in ([0, 1] if unit == 0 else [unit + 1]):
            for part in range(PARTS):
                across(s, part).wait_recv()
        for kk in range(PER_UNIT):
            slot = quad + unit * PER_UNIT + 1 + kk
            spot = slot % 4
            b_spec[:, kk] = b_land[slot // 4, spot % 2, spot // 2].astype(F32)
        low, high = products(cross_unit, ROWS)
        prod[:, :HALF] = dot(low, flip_ref[:HALF]).astype(BF16)
        prod[:, HALF:] = high
        rows = dot(send_ref[: BANDS * (MAIN + 16)], prod[...])
        main = rows[: BANDS * MAIN].astype(BF16).reshape(BANDS, 2, 16, LAGS)
        s_main[unit, :, :, :LAGS] = main[:, 0]
        s_main[unit, :, :, LAGS : 2 * LAGS] = main[:, 1]
        rows = rows[BANDS * MAIN :]
        left = rows[:, :128]
        for t in range(1, 4):
            left = jnp.where(tile == t, rows[:, t * 128 : t * 128 + 128], left)
        s_main[unit, :, :, 2 * LAGS :] = left.astype(BF16).reshape(BANDS, 16, 128)
        for copy in out_copies(unit):
            copy.start()
        kept(unit).start()

    low, high = products(cross_own, 96)
    low = dot(low, flip_ref[:HALF])
    value = jnp.concatenate([low, high.astype(F32)], axis=1)[:72]
    row = lax.broadcasted_iota(jnp.int32, (72, LAGS), 0)
    mine = row // STA + OWN * freq
    own[...] = jnp.where(row % STA != mine, value, 0.0).reshape(OWN, STA, LAGS).astype(BF16)
    own_copy = pltpu.make_async_copy(own, own_out, own_sem)
    own_copy.start()

    for unit in range(UNITS):
        for copy in out_copies(unit):
            copy.wait_recv()
        kept(unit).wait()
    own_copy.wait()
    for copy in b_copies + a_copies:
        copy.wait_send()
    for unit in range(UNITS):
        for copy in out_copies(unit):
            copy.wait_send()
        if unit > 0:
            for part in range(PARTS):
                ring(unit, part).wait_send()
    for s in range(UNITS + 1):
        for part in range(PARTS):
            across(s, part).wait_send()


def assemble(m_hbm, own_hbm, mask_hbm, main_hbm, left_hbm, out_hbm, m, mask, main_ref, left_ref, done, in_sem, out_sem):
    sta = lax.axis_index("sta")
    sources = [main_hbm, left_hbm, mask_hbm] + [m_hbm.at[unit] for unit in range(UNITS)]
    targets = [main_ref, left_ref, mask] + [m.at[unit] for unit in range(UNITS)]
    fetches = [pltpu.make_async_copy(a, b, in_sem.at[n]) for n, (a, b) in enumerate(zip(sources, targets))]
    for fetch in fetches:
        fetch.start()
    stores = [pltpu.make_async_copy(own_hbm, out_hbm.at[0], out_sem.at[UNITS])]
    stores[0].start()
    for fetch in fetches[:3]:
        fetch.wait()
    for unit in range(UNITS):
        fetches[3 + unit].wait()
        halves = [m[unit, :, :, half * LAGS : half * LAGS + LAGS].reshape(BANDS * 16, LAGS) for half in range(2)]
        rows = dot(main_ref[:ROWS], jnp.concatenate(halves, axis=0))
        left = dot(left_ref[: 4 * 72], m[unit, :, :, 2 * LAGS :].reshape(BANDS * 16, 128))
        left = jnp.concatenate([left[t * 72 : t * 72 + 72] for t in range(4)], axis=1)
        for kk in range(PER_UNIT):
            value = rows[kk * 72 : kk * 72 + 72]
            if kk == PER_UNIT - 1:
                value = value + left
            on = mask[sta, (sta + unit * PER_UNIT + 1 + kk) % 32] > 0
            done[unit, kk] = jnp.where(on, value, 0.0).reshape(OWN, STA, LAGS).astype(BF16)
        store = pltpu.make_async_copy(done.at[unit], out_hbm.at[pl.ds(1 + unit * PER_UNIT, PER_UNIT)], out_sem.at[unit])
        store.start()
        stores.append(store)
    for store in stores:
        store.wait()


def local(spectra, pair_mask):
    main, left = final_select()
    arrays = [spectra, padded(piece_select()), phases(), padded(half_tables()), padded(send_select()), padded(flip())]
    dma = pltpu.SemaphoreType.DMA
    anywhere = pl.BlockSpec(memory_space=pl.ANY)
    held, own = pl.pallas_call(
        kernel,
        out_shape=[
            jax.ShapeDtypeStruct((UNITS, BANDS, 16, WIDE), BF16),
            jax.ShapeDtypeStruct((OWN, STA, LAGS), BF16),
        ],
        in_specs=[anywhere] * INPUTS,
        out_specs=[anywhere] * 2,
        scratch_shapes=[
            *[pltpu.VMEM(value.shape, value.dtype) for value in arrays],
            pltpu.VMEM((BANDS, 16, 256), BF16),
            pltpu.VMEM((UNITS + 1, 2, 2, BANDS, 16, 256), BF16),
            pltpu.VMEM((BANDS, 2, STA, BAND), BF16),
            pltpu.VMEM((BANDS, 2, STA, BAND), F32),
            pltpu.VMEM((BANDS, PER_UNIT, 16, 256), F32),
            pltpu.VMEM((ROWS, BAND), BF16),
            pltpu.VMEM((ROWS, BAND), BF16),
            pltpu.VMEM((ROWS, BAND), BF16),
            pltpu.VMEM((ROWS, BAND), BF16),
            pltpu.VMEM((ROWS, LAGS), F32),
            pltpu.VMEM((ROWS, LAGS), BF16),
            pltpu.VMEM((UNITS, BANDS, 16, WIDE), BF16),
            pltpu.VMEM((OWN, STA, LAGS), BF16),
            dma((INPUTS,)),
            dma((31,)),
            dma((31,)),
            dma((7,)),
            dma((7,)),
            dma((UNITS, PARTS)),
            dma((UNITS, PARTS)),
            dma((UNITS + 1, PARTS)),
            dma((UNITS + 1, PARTS)),
            dma((UNITS, 7)),
            dma((UNITS, 7)),
            dma((UNITS,)),
            dma,
        ],
        compiler_params=pltpu.CompilerParams(
            collective_id=0, has_side_effects=True, vmem_limit_bytes=60 * 1024 * 1024
        ),
        cost_estimate=pl.CostEstimate(flops=10_000_000_000, bytes_accessed=8_000_000, transcendentals=0),
        name="correlate",
    )(*[jnp.asarray(value) for value in arrays])
    selects = [padded(main), padded(left)]
    out = pl.pallas_call(
        assemble,
        out_shape=jax.ShapeDtypeStruct((17, OWN, STA, LAGS), BF16),
        in_specs=[anywhere] * 5,
        out_specs=anywhere,
        scratch_shapes=[
            pltpu.VMEM((UNITS, BANDS, 16, WIDE), BF16),
            pltpu.SMEM(pair_mask.shape, jnp.int32),
            *[pltpu.VMEM(value.shape, value.dtype) for value in selects],
            pltpu.VMEM((UNITS, PER_UNIT, OWN, STA, LAGS), BF16),
            dma((3 + UNITS,)),
            dma((UNITS + 1,)),
        ],
        compiler_params=pltpu.CompilerParams(vmem_limit_bytes=60 * 1024 * 1024),
        cost_estimate=pl.CostEstimate(flops=1_000_000_000, bytes_accessed=4_000_000, transcendentals=0),
        name="assemble",
    )(held, own, pair_mask, *[jnp.asarray(value) for value in selects])
    return out[None]


def solution(mesh):
    return jax.shard_map(
        local,
        mesh=mesh,
        in_specs=(P(None, "sta", "freq"), P()),
        out_specs=P("sta", None, "freq", None, None),
        check_vma=False,
    )
```

```python
import functools
import math

import jax
import jax.numpy as jnp
import ml_dtypes
import numpy as np
from jax import lax
from jax.experimental import pallas as pl
from jax.experimental.pallas import tpu as pltpu
from jax.sharding import PartitionSpec as P

FREQS = 4096
LAGS = 512
HALF = LAGS // 2
STA = 24
BAND = 512
BANDS = 8
OWN = 3
UNITS = 4
PER_UNIT = 4
PAIRS = PER_UNIT * OWN
ROWS = PAIRS * STA
MAIN = 32
LEFT = 4
WIDE = 2 * LAGS + 128
INPUTS = 6
PARTS = 4
PACKED = 12 * BANDS
MESH = pl.DeviceIdType.MESH
F32 = jnp.float32
BF16 = jnp.bfloat16


def half_tables():
    bins = np.arange(FREQS, dtype=np.float64)[:, None]
    lags = np.arange(HALF, dtype=np.float64)[None, :] + 0.5
    angle = math.pi * bins * lags / FREQS
    both = np.concatenate([np.cos(angle), np.sin(angle)], axis=1) / math.sqrt(FREQS)
    return both.astype(np.float32).astype(ml_dtypes.bfloat16).reshape(BANDS, BAND, LAGS)


def padded(value):
    return np.pad(value, [(0, 0)] * (value.ndim - 2) + [(0, 8), (0, 0)])


def phases():
    angle = math.pi * np.arange(FREQS, dtype=np.float64) / (2 * FREQS)
    both = np.stack([np.cos(angle), np.sin(angle)])
    return both.reshape(2 * BANDS, 1, BAND).astype(np.float32)


def piece_select():
    select = np.zeros((4, BANDS * 16, STA), np.float32)
    for dest in range(BANDS):
        for jj in range(OWN):
            for part in range(2):
                for half in range(2):
                    row = dest * 16 + (jj * 2 + part) * 2 + half
                    select[part * 2 + half, row, OWN * dest + jj] = 1
    return select.astype(ml_dtypes.bfloat16)


def send_select():
    select = np.zeros((BANDS * (MAIN + 16), ROWS), np.float32)
    for dest in range(BANDS):
        for kk in range(PER_UNIT):
            for il in range(OWN):
                for jj in range(OWN):
                    r = kk * 9 + il * OWN + jj
                    column = (kk * OWN + jj) * STA + OWN * dest + il
                    if r < MAIN:
                        select[dest * MAIN + r, column] = 1
                    else:
                        for tile in range(4):
                            select[BANDS * MAIN + dest * 16 + tile * LEFT + r - MAIN, column] = 1
    return select.astype(ml_dtypes.bfloat16)


def final_select():
    main = np.zeros((ROWS, BANDS * MAIN), np.float32)
    left = np.zeros((4 * 72, BANDS * 16), np.float32)
    for source in range(BANDS):
        for kk in range(PER_UNIT):
            for il in range(OWN):
                for jj in range(OWN):
                    r = kk * 9 + il * OWN + jj
                    row = il * STA + OWN * source + jj
                    if r < MAIN:
                        main[kk * 72 + row, r // 16 * 128 + source * 16 + r % 16] = 1
                    else:
                        for tile in range(4):
                            left[tile * 72 + row, source * 16 + tile * LEFT + r - MAIN] = 1
    return main.astype(ml_dtypes.bfloat16), left.astype(ml_dtypes.bfloat16)


def flip():
    return np.eye(HALF, dtype=np.float32)[::-1].astype(ml_dtypes.bfloat16)


def dot(a, b):
    return jnp.dot(a, b, preferred_element_type=F32)


def kernel(
    *refs,
):
    inputs, m_out, own_out, refs = refs[:INPUTS], refs[INPUTS], refs[INPUTS + 1], refs[INPUTS + 2 :]
    held, refs = refs[:INPUTS], refs[INPUTS:]
    x_ref, piece_ref, phase_ref, table, send_ref, flip_ref = held
    (
    pieces, p_land, b_land, a_land, a_spec, b_spec, lre0, lim0, lre1, lim1, acc, prod, s_main, own,
    in_sem, b_send, b_recv, a_send, a_recv, ring_send, ring_recv, sib_send, sib_recv, o_send, o_recv, m_sem, own_sem,
    ) = refs
    sta, freq = lax.axis_index("sta"), lax.axis_index("freq")
    z, quad = sta // 4, sta % 4
    ylo, core = quad // 2, quad % 2
    xx, yhi = freq // 2, freq % 2

    fetches = [pltpu.make_async_copy(inputs[n], held[n], in_sem.at[n]) for n in range(INPUTS)]
    for fetch in fetches:
        fetch.start()

    def peer(dx, dh, dl, dz=0):
        return (
            (z + 8 - dz) % 8 * 4 + (ylo + dl) % 2 * 2 + core,
            (xx + dx) % 4 * 2 + (yhi + dh) % 2,
        )

    plane = [(dx, dh, dl) for dl in range(2) for dh in range(2) for dx in range(4)]
    plane.sort(key=lambda d: -(min(d[0], 4 - d[0]) + 2 * d[1] + d[2]))
    others = plane[:-1]
    group = [d for d in others if d[2] == 0]
    below = ((sta + 28) % 32, freq)
    nearby = [(*d, 0) for d in others] + [(*d, 1) for d in plane]
    sibling = (z * 4 + ylo * 2 + (1 - core), freq)

    barrier = pltpu.get_barrier_semaphore()
    for device in [peer(dx, dh, dl, -dz) for dx, dh, dl, dz in nearby] + [sibling]:
        pl.semaphore_signal(barrier, inc=1, device_id=device, device_id_type=MESH)

    fetches[0].wait()
    fetches[1].wait()
    total = None
    for part in range(2):
        for half in range(2):
            term = dot(piece_ref[part * 2 + half, :128], x_ref[part, :, half * 256 : half * 256 + 256])
            total = term if total is None else total + term
    pieces[...] = total.astype(BF16).reshape(BANDS, 16, 256)

    pl.semaphore_wait(barrier, len(nearby) + 1)

    def remote(src, dst, send, recv, device):
        return pltpu.make_async_remote_copy(
            src_ref=src, dst_ref=dst, send_sem=send, recv_sem=recv, device_id=device, device_id_type=MESH
        )

    b_copies = []
    for n, d in enumerate(nearby):
        device = peer(*d)
        b_copies.append(
            remote(pieces.at[device[1]], p_land.at[d[3], ylo, freq], b_send.at[n], b_recv.at[n], device)
        )
    a_copies = []
    for n, d in enumerate(group):
        a_copies.append(remote(x_ref, a_land.at[freq], a_send.at[n], a_recv.at[n], peer(*d)))
    for copy in b_copies + a_copies:
        copy.start()
    p_land[0, ylo, freq] = pieces[freq]
    a_land[freq] = x_ref[...]

    def ring(s, part):
        y, h = part // 2, pl.ds(part % 2 * 48, 48)
        return remote(
            b_land.at[s, core, y, h], b_land.at[s + 1, core, y, h], ring_send.at[s, part], ring_recv.at[s, part], below
        )

    def across(s, part):
        y, h = part // 2, pl.ds(part % 2 * 48, 48)
        return remote(
            b_land.at[s, core, y, h], b_land.at[s, core, y, h], sib_send.at[s, part], sib_recv.at[s, part], sibling
        )

    def forward(s):
        for part in range(PARTS):
            if s > 1:
                ring(s - 1, part).wait_recv()
            if 0 < s < UNITS:
                ring(s, part).start()
            across(s, part).start()

    for copy in b_copies:
        copy.wait_recv()
    row = lax.broadcasted_iota(jnp.int32, (PACKED, BANDS * 16), 0)
    column = lax.broadcasted_iota(jnp.int32, (PACKED, BANDS * 16), 1)
    pack = jnp.where(column == row % BANDS * 16 + row // BANDS, 1.0, 0.0).astype(BF16)
    for s in (1, 0):
        for y in range(2):
            b_land[s, core, y] = dot(pack, p_land[s, y].reshape(BANDS * 16, 256)).astype(BF16)
        forward(s)

    for copy in a_copies:
        copy.wait_recv()

    def rotate(h, carry):
        cos, sin = phase_ref[h], phase_ref[BANDS + h]
        re = a_land[h, 0].astype(F32)
        im = a_land[h, 1].astype(F32)
        a_spec[h, 0] = re * cos + im * sin
        a_spec[h, 1] = im * cos - re * sin
        return carry

    fetches[2].wait()
    lax.fori_loop(0, BANDS, rotate, 0)
    for fetch in fetches[3:]:
        fetch.wait()

    def products(cross, rows):
        buffers = ((lre0, lim0), (lre1, lim1))

        def fill(two):
            for e in range(2):
                cross(2 * two + e, buffers[two % 2], e * BAND)

        def project(two):
            for n, part in enumerate(buffers[two % 2]):
                columns = slice(n * HALF, n * HALF + HALF)
                basis = table[2 * two : 2 * two + 2, :BAND, columns].reshape(2 * BAND, HALF)
                term = dot(part[:rows], basis)
                acc[:rows, columns] = term if two == 0 else acc[:rows, columns] + term

        fill(0)
        for two in range(BANDS // 2):
            if two + 1 < BANDS // 2:
                fill(two + 1)
            project(two)
        cos, sin = acc[:rows, :HALF], acc[:rows, HALF:]
        return (cos + sin).astype(BF16), (cos - sin).astype(BF16)

    def cross_unit(h, buffers, start):
        for half in range(2):
            lanes = slice(half * 256, half * 256 + 256)
            place = slice(start + half * 256, start + half * 256 + 256)
            ar, ai = a_spec[h, 0, :, lanes], a_spec[h, 1, :, lanes]
            for two in range(PAIRS // 2):
                re, im = [], []
                for g in (2 * two, 2 * two + 1):
                    kk, jj = g // OWN, g % OWN
                    row = jj * 4 + half
                    br = b_spec[kk, row, h : h + 1, :]
                    bi = b_spec[kk, row + 2, h : h + 1, :]
                    re.append(ar * br + ai * bi)
                    im.append(ai * br - ar * bi)
                buffers[0][two * 48 : two * 48 + 48, place] = jnp.concatenate(re, axis=0).astype(BF16)
                buffers[1][two * 48 : two * 48 + 48, place] = jnp.concatenate(im, axis=0).astype(BF16)

    def cross_own(h, buffers, start):
        for half in range(2):
            lanes = slice(half * 256, half * 256 + 256)
            place = slice(start + half * 256, start + half * 256 + 256)
            br = a_land[h, 0, :, lanes].astype(F32)
            bi = a_land[h, 1, :, lanes].astype(F32)
            re, im = [], []
            for il in (0, 1, 2, 2):
                ar = a_spec[h, 0, pl.ds(OWN * freq + il, 1), lanes]
                ai = a_spec[h, 1, pl.ds(OWN * freq + il, 1), lanes]
                re.append(ar * br + ai * bi)
                im.append(ai * br - ar * bi)
            buffers[0][:96, place] = jnp.concatenate(re, axis=0).astype(BF16)
            buffers[1][:96, place] = jnp.concatenate(im, axis=0).astype(BF16)

    def out_copies(unit):
        copies = []
        for n, d in enumerate(group):
            device = peer(*d)
            copies.append(
                remote(s_main.at[unit, device[1]], m_out.at[unit, freq], o_send.at[unit, n], o_recv.at[unit, n], device)
            )
        return copies

    def kept(unit):
        return pltpu.make_async_copy(s_main.at[unit, freq], m_out.at[unit, freq], m_sem.at[unit])

    tile = lax.broadcasted_iota(jnp.int32, (BANDS * 16, 128), 0) // LEFT % 4

    for unit in range(UNITS):
        if unit + 2 <= UNITS:
            forward(unit + 2)
        for s in ([0, 1] if unit == 0 else [unit + 1]):
            for part in range(PARTS):
                across(s, part).wait_recv()
        for kk in range(PER_UNIT):
            slot = quad + unit * PER_UNIT + 1 + kk
            spot = slot % 4
            b_spec[kk] = b_land[slot // 4, spot % 2, spot // 2].astype(F32).reshape(12, BANDS, 256)
        low, high = products(cross_unit, ROWS)
        prod[:, :HALF] = dot(low, flip_ref[:HALF]).astype(BF16)
        prod[:, HALF:] = high
        rows = dot(send_ref[: BANDS * (MAIN + 16)], prod[...])
        main = rows[: BANDS * MAIN].astype(BF16).reshape(BANDS, 2, 16, LAGS)
        s_main[unit, :, :, :LAGS] = main[:, 0]
        s_main[unit, :, :, LAGS : 2 * LAGS] = main[:, 1]
        rows = rows[BANDS * MAIN :]
        left = rows[:, :128]
        for t in range(1, 4):
            left = jnp.where(tile == t, rows[:, t * 128 : t * 128 + 128], left)
        s_main[unit, :, :, 2 * LAGS :] = left.astype(BF16).reshape(BANDS, 16, 128)
        for copy in out_copies(unit):
            copy.start()
        kept(unit).start()

    low, high = products(cross_own, 96)
    low = dot(low, flip_ref[:HALF])
    value = jnp.concatenate([low, high.astype(F32)], axis=1)[:72]
    row = lax.broadcasted_iota(jnp.int32, (72, LAGS), 0)
    mine = row // STA + OWN * freq
    own[...] = jnp.where(row % STA != mine, value, 0.0).reshape(OWN, STA, LAGS).astype(BF16)
    own_copy = pltpu.make_async_copy(own, own_out, own_sem)
    own_copy.start()

    for unit in range(UNITS):
        for copy in out_copies(unit):
            copy.wait_recv()
        kept(unit).wait()
    own_copy.wait()
    for copy in b_copies + a_copies:
        copy.wait_send()
    for unit in range(UNITS):
        for copy in out_copies(unit):
            copy.wait_send()
        if unit > 0:
            for part in range(PARTS):
                ring(unit, part).wait_send()
    for s in range(UNITS + 1):
        for part in range(PARTS):
            across(s, part).wait_send()


def assemble(m_hbm, own_hbm, mask_hbm, main_hbm, left_hbm, out_hbm, m, mask, main_ref, left_ref, own, done, in_sem, out_sem):
    sta = lax.axis_index("sta")
    sources = [main_hbm, left_hbm, mask_hbm, own_hbm] + [m_hbm.at[unit] for unit in range(UNITS)]
    targets = [main_ref, left_ref, mask, own] + [m.at[unit] for unit in range(UNITS)]
    fetches = [pltpu.make_async_copy(a, b, in_sem.at[n]) for n, (a, b) in enumerate(zip(sources, targets))]
    for fetch in fetches:
        fetch.start()
    for fetch in fetches[:4]:
        fetch.wait()
    stores = [pltpu.make_async_copy(own, out_hbm.at[0], out_sem.at[UNITS])]
    stores[0].start()
    for unit in range(UNITS):
        fetches[4 + unit].wait()
        halves = [m[unit, :, :, half * LAGS : half * LAGS + LAGS].reshape(BANDS * 16, LAGS) for half in range(2)]
        rows = dot(main_ref[:ROWS], jnp.concatenate(halves, axis=0))
        left = dot(left_ref[: 4 * 72], m[unit, :, :, 2 * LAGS :].reshape(BANDS * 16, 128))
        left = jnp.concatenate([left[t * 72 : t * 72 + 72] for t in range(4)], axis=1)
        for kk in range(PER_UNIT):
            value = rows[kk * 72 : kk * 72 + 72]
            if kk == PER_UNIT - 1:
                value = value + left
            on = mask[sta, (sta + unit * PER_UNIT + 1 + kk) % 32] > 0
            done[unit, kk] = jnp.where(on, value, 0.0).reshape(OWN, STA, LAGS).astype(BF16)
        store = pltpu.make_async_copy(done.at[unit], out_hbm.at[pl.ds(1 + unit * PER_UNIT, PER_UNIT)], out_sem.at[unit])
        store.start()
        stores.append(store)
    for store in stores:
        store.wait()


def local(spectra, pair_mask):
    main, left = final_select()
    arrays = [spectra, padded(piece_select()), phases(), padded(half_tables()), padded(send_select()), padded(flip())]
    dma = pltpu.SemaphoreType.DMA
    anywhere = pl.BlockSpec(memory_space=pl.ANY)
    held, own = pl.pallas_call(
        kernel,
        out_shape=[
            jax.ShapeDtypeStruct((UNITS, BANDS, 16, WIDE), BF16),
            jax.ShapeDtypeStruct((OWN, STA, LAGS), BF16),
        ],
        in_specs=[anywhere] * INPUTS,
        out_specs=[anywhere] * 2,
        scratch_shapes=[
            *[pltpu.VMEM(value.shape, value.dtype) for value in arrays],
            pltpu.VMEM((BANDS, 16, 256), BF16),
            pltpu.VMEM((2, 2, BANDS, 16, 256), BF16),
            pltpu.VMEM((UNITS + 1, 2, 2, PACKED, 256), BF16),
            pltpu.VMEM((BANDS, 2, STA, BAND), BF16),
            pltpu.VMEM((BANDS, 2, STA, BAND), F32),
            pltpu.VMEM((PER_UNIT, 12, BANDS, 256), F32),
            pltpu.VMEM((ROWS, 2 * BAND), BF16),
            pltpu.VMEM((ROWS, 2 * BAND), BF16),
            pltpu.VMEM((ROWS, 2 * BAND), BF16),
            pltpu.VMEM((ROWS, 2 * BAND), BF16),
            pltpu.VMEM((ROWS, LAGS), F32),
            pltpu.VMEM((ROWS, LAGS), BF16),
            pltpu.VMEM((UNITS, BANDS, 16, WIDE), BF16),
            pltpu.VMEM((OWN, STA, LAGS), BF16),
            dma((INPUTS,)),
            dma((31,)),
            dma((31,)),
            dma((7,)),
            dma((7,)),
            dma((UNITS, PARTS)),
            dma((UNITS, PARTS)),
            dma((UNITS + 1, PARTS)),
            dma((UNITS + 1, PARTS)),
            dma((UNITS, 7)),
            dma((UNITS, 7)),
            dma((UNITS,)),
            dma,
        ],
        compiler_params=pltpu.CompilerParams(
            collective_id=0, has_side_effects=True, vmem_limit_bytes=60 * 1024 * 1024
        ),
        cost_estimate=pl.CostEstimate(flops=10_000_000_000, bytes_accessed=8_000_000, transcendentals=0),
        name="correlate",
    )(*[jnp.asarray(value) for value in arrays])
    selects = [padded(main), padded(left)]
    out = pl.pallas_call(
        assemble,
        out_shape=jax.ShapeDtypeStruct((17, OWN, STA, LAGS), BF16),
        in_specs=[anywhere] * 5,
        out_specs=anywhere,
        scratch_shapes=[
            pltpu.VMEM((UNITS, BANDS, 16, WIDE), BF16),
            pltpu.SMEM(pair_mask.shape, jnp.int32),
            *[pltpu.VMEM(value.shape, value.dtype) for value in selects],
            pltpu.VMEM((OWN, STA, LAGS), BF16),
            pltpu.VMEM((UNITS, PER_UNIT, OWN, STA, LAGS), BF16),
            dma((4 + UNITS,)),
            dma((UNITS + 1,)),
        ],
        compiler_params=pltpu.CompilerParams(vmem_limit_bytes=60 * 1024 * 1024),
        cost_estimate=pl.CostEstimate(flops=1_000_000_000, bytes_accessed=4_000_000, transcendentals=0),
        name="assemble",
    )(held, own, pair_mask, *[jnp.asarray(value) for value in selects])
    return out[None]


def solution(mesh):
    return jax.shard_map(
        local,
        mesh=mesh,
        in_specs=(P(None, "sta", "freq"), P()),
        out_specs=P("sta", None, "freq", None, None),
        check_vma=False,
    )
```

```python
import functools
import math

import jax
import jax.numpy as jnp
import ml_dtypes
import numpy as np
from jax import lax
from jax.experimental import pallas as pl
from jax.experimental.pallas import tpu as pltpu
from jax.sharding import PartitionSpec as P

FREQS = 4096
LAGS = 512
HALF = LAGS // 2
STA = 24
BAND = 512
BANDS = 8
OWN = 3
UNITS = 4
PER_UNIT = 4
PAIRS = PER_UNIT * OWN
ROWS = PAIRS * STA
MAIN = 32
LEFT = 4
WIDE = 2 * LAGS + 128
INPUTS = 6
PARTS = 4
PACKED = 12 * BANDS
MESH = pl.DeviceIdType.MESH
F32 = jnp.float32
BF16 = jnp.bfloat16


def half_tables():
    bins = np.arange(FREQS, dtype=np.float64)[:, None]
    lags = np.arange(HALF, dtype=np.float64)[None, :] + 0.5
    angle = math.pi * bins * lags / FREQS
    both = np.concatenate([np.cos(angle), np.sin(angle)], axis=1) / math.sqrt(FREQS)
    return both.astype(np.float32).astype(ml_dtypes.bfloat16).reshape(BANDS, BAND, LAGS)


def padded(value):
    return np.pad(value, [(0, 0)] * (value.ndim - 2) + [(0, 8), (0, 0)])


def phases():
    angle = math.pi * np.arange(FREQS, dtype=np.float64) / (2 * FREQS)
    both = np.stack([np.cos(angle), np.sin(angle)])
    return both.reshape(2 * BANDS, 1, BAND).astype(np.float32)


def piece_select():
    select = np.zeros((4, BANDS * 16, STA), np.float32)
    for dest in range(BANDS):
        for jj in range(OWN):
            for part in range(2):
                for half in range(2):
                    row = dest * 16 + (jj * 2 + part) * 2 + half
                    select[part * 2 + half, row, OWN * dest + jj] = 1
    return select.astype(ml_dtypes.bfloat16)


def send_select():
    select = np.zeros((BANDS * (MAIN + 16), ROWS), np.float32)
    for dest in range(BANDS):
        for kk in range(PER_UNIT):
            for il in range(OWN):
                for jj in range(OWN):
                    r = kk * 9 + il * OWN + jj
                    column = (kk * OWN + jj) * STA + OWN * dest + il
                    if r < MAIN:
                        select[dest * MAIN + r, column] = 1
                    else:
                        for tile in range(4):
                            select[BANDS * MAIN + dest * 16 + tile * LEFT + r - MAIN, column] = 1
    return select.astype(ml_dtypes.bfloat16)


def final_select():
    main = np.zeros((ROWS, BANDS * MAIN), np.float32)
    left = np.zeros((4 * 72, BANDS * 16), np.float32)
    for source in range(BANDS):
        for kk in range(PER_UNIT):
            for il in range(OWN):
                for jj in range(OWN):
                    r = kk * 9 + il * OWN + jj
                    row = il * STA + OWN * source + jj
                    if r < MAIN:
                        main[kk * 72 + row, r // 16 * 128 + source * 16 + r % 16] = 1
                    else:
                        for tile in range(4):
                            left[tile * 72 + row, source * 16 + tile * LEFT + r - MAIN] = 1
    return main.astype(ml_dtypes.bfloat16), left.astype(ml_dtypes.bfloat16)


def flip():
    return np.eye(HALF, dtype=np.float32)[::-1].astype(ml_dtypes.bfloat16)


def dot(a, b):
    return jnp.dot(a, b, preferred_element_type=F32)


def kernel(
    *refs,
):
    inputs, m_out, own_out, refs = refs[:INPUTS], refs[INPUTS], refs[INPUTS + 1], refs[INPUTS + 2 :]
    held, refs = refs[:INPUTS], refs[INPUTS:]
    x_ref, piece_ref, phase_ref, table, send_ref, flip_ref = held
    (
    pieces, p_land, b_land, a_land, a_spec, b_spec, lre0, lim0, lre1, lim1, acc, prod, s_main, own,
    in_sem, b_send, b_recv, a_send, a_recv, ring_send, ring_recv, sib_send, sib_recv, o_send, o_recv, m_sem, own_sem,
    ) = refs
    sta, freq = lax.axis_index("sta"), lax.axis_index("freq")
    z, quad = sta // 4, sta % 4
    ylo, core = quad // 2, quad % 2
    xx, yhi = freq // 2, freq % 2

    fetches = [pltpu.make_async_copy(inputs[n], held[n], in_sem.at[n]) for n in range(INPUTS)]
    for fetch in fetches[:2]:
        fetch.start()

    def peer(dx, dh, dl, dz=0):
        return (
            (z + 8 - dz) % 8 * 4 + (ylo + dl) % 2 * 2 + core,
            (xx + dx) % 4 * 2 + (yhi + dh) % 2,
        )

    plane = [(dx, dh, dl) for dl in range(2) for dh in range(2) for dx in range(4)]
    plane.sort(key=lambda d: -(min(d[0], 4 - d[0]) + 2 * d[1] + d[2]))
    others = plane[:-1]
    group = [d for d in others if d[2] == 0]
    below = ((sta + 28) % 32, freq)
    nearby = [(*d, 1) for d in plane] + [(*d, 0) for d in others]
    sibling = (z * 4 + ylo * 2 + (1 - core), freq)

    barrier = pltpu.get_barrier_semaphore()
    for device in [peer(dx, dh, dl, -dz) for dx, dh, dl, dz in nearby] + [sibling]:
        pl.semaphore_signal(barrier, inc=1, device_id=device, device_id_type=MESH)

    for fetch in fetches[2:]:
        fetch.start()
    fetches[0].wait()
    fetches[1].wait()
    total = None
    for part in range(2):
        for half in range(2):
            term = dot(piece_ref[part * 2 + half, :128], x_ref[part, :, half * 256 : half * 256 + 256])
            total = term if total is None else total + term
    pieces[...] = total.astype(BF16).reshape(BANDS, 16, 256)

    pl.semaphore_wait(barrier, len(nearby) + 1)

    def remote(src, dst, send, recv, device):
        return pltpu.make_async_remote_copy(
            src_ref=src, dst_ref=dst, send_sem=send, recv_sem=recv, device_id=device, device_id_type=MESH
        )

    b_copies = []
    for n, d in enumerate(nearby):
        device = peer(*d)
        b_copies.append(
            remote(pieces.at[device[1]], p_land.at[d[3], ylo, freq], b_send.at[n], b_recv.at[n], device)
        )
    a_copies = []
    for n, d in enumerate(group):
        a_copies.append(remote(x_ref, a_land.at[freq], a_send.at[n], a_recv.at[n], peer(*d)))
    for copy in b_copies + a_copies:
        copy.start()
    p_land[0, ylo, freq] = pieces[freq]
    a_land[freq] = x_ref[...]

    def ring(s, part):
        y, h = part // 2, pl.ds(part % 2 * 48, 48)
        return remote(
            b_land.at[s, core, y, h], b_land.at[s + 1, core, y, h], ring_send.at[s, part], ring_recv.at[s, part], below
        )

    def across(s, part):
        y, h = part // 2, pl.ds(part % 2 * 48, 48)
        return remote(
            b_land.at[s, core, y, h], b_land.at[s, core, y, h], sib_send.at[s, part], sib_recv.at[s, part], sibling
        )

    def forward(s):
        for part in range(PARTS):
            if s > 1:
                ring(s - 1, part).wait_recv()
            if 0 < s < UNITS:
                ring(s, part).start()
            across(s, part).start()

    row = lax.broadcasted_iota(jnp.int32, (PACKED, BANDS * 16), 0)
    column = lax.broadcasted_iota(jnp.int32, (PACKED, BANDS * 16), 1)
    pack = jnp.where(column == row % BANDS * 16 + row // BANDS, 1.0, 0.0).astype(BF16)
    for s in (1, 0):
        for d, copy in zip(nearby, b_copies):
            if d[3] == s:
                copy.wait_recv()
        for y in range(2):
            b_land[s, core, y] = dot(pack, p_land[s, y].reshape(BANDS * 16, 256)).astype(BF16)
        forward(s)

    for copy in a_copies:
        copy.wait_recv()

    def rotate(h, carry):
        cos, sin = phase_ref[h], phase_ref[BANDS + h]
        re = a_land[h, 0].astype(F32)
        im = a_land[h, 1].astype(F32)
        a_spec[h, 0] = re * cos + im * sin
        a_spec[h, 1] = im * cos - re * sin
        return carry

    fetches[2].wait()
    lax.fori_loop(0, BANDS, rotate, 0)
    for fetch in fetches[3:]:
        fetch.wait()

    def products(cross, rows):
        buffers = ((lre0, lim0), (lre1, lim1))

        def fill(two):
            for e in range(2):
                cross(2 * two + e, buffers[two % 2], e * BAND)

        def project(two):
            for n, part in enumerate(buffers[two % 2]):
                columns = slice(n * HALF, n * HALF + HALF)
                basis = table[2 * two : 2 * two + 2, :BAND, columns].reshape(2 * BAND, HALF)
                term = dot(part[:rows], basis)
                acc[:rows, columns] = term if two == 0 else acc[:rows, columns] + term

        fill(0)
        for two in range(BANDS // 2):
            if two + 1 < BANDS // 2:
                fill(two + 1)
            project(two)
        cos, sin = acc[:rows, :HALF], acc[:rows, HALF:]
        return (cos + sin).astype(BF16), (cos - sin).astype(BF16)

    def cross_unit(h, buffers, start):
        for half in range(2):
            lanes = slice(half * 256, half * 256 + 256)
            place = slice(start + half * 256, start + half * 256 + 256)
            ar, ai = a_spec[h, 0, :, lanes], a_spec[h, 1, :, lanes]
            for two in range(PAIRS // 2):
                re, im = [], []
                for g in (2 * two, 2 * two + 1):
                    kk, jj = g // OWN, g % OWN
                    row = jj * 4 + half
                    br = b_spec[kk, row, h : h + 1, :]
                    bi = b_spec[kk, row + 2, h : h + 1, :]
                    re.append(ar * br + ai * bi)
                    im.append(ai * br - ar * bi)
                buffers[0][two * 48 : two * 48 + 48, place] = jnp.concatenate(re, axis=0).astype(BF16)
                buffers[1][two * 48 : two * 48 + 48, place] = jnp.concatenate(im, axis=0).astype(BF16)

    def cross_own(h, buffers, start):
        for half in range(2):
            lanes = slice(half * 256, half * 256 + 256)
            place = slice(start + half * 256, start + half * 256 + 256)
            br = a_land[h, 0, :, lanes].astype(F32)
            bi = a_land[h, 1, :, lanes].astype(F32)
            re, im = [], []
            for il in (0, 1, 2, 2):
                ar = a_spec[h, 0, pl.ds(OWN * freq + il, 1), lanes]
                ai = a_spec[h, 1, pl.ds(OWN * freq + il, 1), lanes]
                re.append(ar * br + ai * bi)
                im.append(ai * br - ar * bi)
            buffers[0][:96, place] = jnp.concatenate(re, axis=0).astype(BF16)
            buffers[1][:96, place] = jnp.concatenate(im, axis=0).astype(BF16)

    def out_copies(unit):
        copies = []
        for n, d in enumerate(group):
            device = peer(*d)
            copies.append(
                remote(s_main.at[unit, device[1]], m_out.at[unit, freq], o_send.at[unit, n], o_recv.at[unit, n], device)
            )
        return copies

    def kept(unit):
        return pltpu.make_async_copy(s_main.at[unit, freq], m_out.at[unit, freq], m_sem.at[unit])

    tile = lax.broadcasted_iota(jnp.int32, (BANDS * 16, 128), 0) // LEFT % 4

    for unit in range(UNITS):
        if unit + 2 <= UNITS:
            forward(unit + 2)
        for s in ([0, 1] if unit == 0 else [unit + 1]):
            for part in range(PARTS):
                across(s, part).wait_recv()
        for kk in range(PER_UNIT):
            slot = quad + unit * PER_UNIT + 1 + kk
            spot = slot % 4
            b_spec[kk] = b_land[slot // 4, spot % 2, spot // 2].astype(F32).reshape(12, BANDS, 256)
        low, high = products(cross_unit, ROWS)
        prod[:, :HALF] = dot(low, flip_ref[:HALF]).astype(BF16)
        prod[:, HALF:] = high
        rows = dot(send_ref[: BANDS * (MAIN + 16)], prod[...])
        main = rows[: BANDS * MAIN].astype(BF16).reshape(BANDS, 2, 16, LAGS)
        s_main[unit, :, :, :LAGS] = main[:, 0]
        s_main[unit, :, :, LAGS : 2 * LAGS] = main[:, 1]
        rows = rows[BANDS * MAIN :]
        left = rows[:, :128]
        for t in range(1, 4):
            left = jnp.where(tile == t, rows[:, t * 128 : t * 128 + 128], left)
        s_main[unit, :, :, 2 * LAGS :] = left.astype(BF16).reshape(BANDS, 16, 128)
        for copy in out_copies(unit):
            copy.start()
        kept(unit).start()

    low, high = products(cross_own, 96)
    low = dot(low, flip_ref[:HALF])
    value = jnp.concatenate([low, high.astype(F32)], axis=1)[:72]
    row = lax.broadcasted_iota(jnp.int32, (72, LAGS), 0)
    mine = row // STA + OWN * freq
    own[...] = jnp.where(row % STA != mine, value, 0.0).reshape(OWN, STA, LAGS).astype(BF16)
    own_copy = pltpu.make_async_copy(own, own_out, own_sem)
    own_copy.start()

    for unit in range(UNITS):
        for copy in out_copies(unit):
            copy.wait_recv()
        kept(unit).wait()
    own_copy.wait()
    for copy in b_copies + a_copies:
        copy.wait_send()
    for unit in range(UNITS):
        for copy in out_copies(unit):
            copy.wait_send()
        if unit > 0:
            for part in range(PARTS):
                ring(unit, part).wait_send()
    for s in range(UNITS + 1):
        for part in range(PARTS):
            across(s, part).wait_send()


def assemble(m_hbm, own_hbm, mask_hbm, main_hbm, left_hbm, out_hbm, m, mask, main_ref, left_ref, own, done, in_sem, out_sem):
    sta = lax.axis_index("sta")
    sources = [main_hbm, left_hbm, mask_hbm, own_hbm] + [m_hbm.at[unit] for unit in range(UNITS)]
    targets = [main_ref, left_ref, mask, own] + [m.at[unit] for unit in range(UNITS)]
    fetches = [pltpu.make_async_copy(a, b, in_sem.at[n]) for n, (a, b) in enumerate(zip(sources, targets))]
    for fetch in fetches:
        fetch.start()
    for fetch in fetches[:4]:
        fetch.wait()
    stores = [pltpu.make_async_copy(own, out_hbm.at[0], out_sem.at[UNITS])]
    stores[0].start()
    for unit in range(UNITS):
        fetches[4 + unit].wait()
        halves = [m[unit, :, :, half * LAGS : half * LAGS + LAGS].reshape(BANDS * 16, LAGS) for half in range(2)]
        rows = dot(main_ref[:ROWS], jnp.concatenate(halves, axis=0))
        left = dot(left_ref[: 4 * 72], m[unit, :, :, 2 * LAGS :].reshape(BANDS * 16, 128))
        left = jnp.concatenate([left[t * 72 : t * 72 + 72] for t in range(4)], axis=1)
        for kk in range(PER_UNIT):
            value = rows[kk * 72 : kk * 72 + 72]
            if kk == PER_UNIT - 1:
                value = value + left
            on = mask[sta, (sta + unit * PER_UNIT + 1 + kk) % 32] > 0
            done[unit, kk] = jnp.where(on, value, 0.0).reshape(OWN, STA, LAGS).astype(BF16)
        store = pltpu.make_async_copy(done.at[unit], out_hbm.at[pl.ds(1 + unit * PER_UNIT, PER_UNIT)], out_sem.at[unit])
        store.start()
        stores.append(store)
    for store in stores:
        store.wait()


def local(spectra, pair_mask):
    main, left = final_select()
    arrays = [spectra, padded(piece_select()), phases(), padded(half_tables()), padded(send_select()), padded(flip())]
    dma = pltpu.SemaphoreType.DMA
    anywhere = pl.BlockSpec(memory_space=pl.ANY)
    held, own = pl.pallas_call(
        kernel,
        out_shape=[
            jax.ShapeDtypeStruct((UNITS, BANDS, 16, WIDE), BF16),
            jax.ShapeDtypeStruct((OWN, STA, LAGS), BF16),
        ],
        in_specs=[anywhere] * INPUTS,
        out_specs=[anywhere] * 2,
        scratch_shapes=[
            *[pltpu.VMEM(value.shape, value.dtype) for value in arrays],
            pltpu.VMEM((BANDS, 16, 256), BF16),
            pltpu.VMEM((2, 2, BANDS, 16, 256), BF16),
            pltpu.VMEM((UNITS + 1, 2, 2, PACKED, 256), BF16),
            pltpu.VMEM((BANDS, 2, STA, BAND), BF16),
            pltpu.VMEM((BANDS, 2, STA, BAND), F32),
            pltpu.VMEM((PER_UNIT, 12, BANDS, 256), F32),
            pltpu.VMEM((ROWS, 2 * BAND), BF16),
            pltpu.VMEM((ROWS, 2 * BAND), BF16),
            pltpu.VMEM((ROWS, 2 * BAND), BF16),
            pltpu.VMEM((ROWS, 2 * BAND), BF16),
            pltpu.VMEM((ROWS, LAGS), F32),
            pltpu.VMEM((ROWS, LAGS), BF16),
            pltpu.VMEM((UNITS, BANDS, 16, WIDE), BF16),
            pltpu.VMEM((OWN, STA, LAGS), BF16),
            dma((INPUTS,)),
            dma((31,)),
            dma((31,)),
            dma((7,)),
            dma((7,)),
            dma((UNITS, PARTS)),
            dma((UNITS, PARTS)),
            dma((UNITS + 1, PARTS)),
            dma((UNITS + 1, PARTS)),
            dma((UNITS, 7)),
            dma((UNITS, 7)),
            dma((UNITS,)),
            dma,
        ],
        compiler_params=pltpu.CompilerParams(
            collective_id=0, has_side_effects=True, vmem_limit_bytes=60 * 1024 * 1024
        ),
        cost_estimate=pl.CostEstimate(flops=10_000_000_000, bytes_accessed=8_000_000, transcendentals=0),
        name="correlate",
    )(*[jnp.asarray(value) for value in arrays])
    selects = [padded(main), padded(left)]
    out = pl.pallas_call(
        assemble,
        out_shape=jax.ShapeDtypeStruct((17, OWN, STA, LAGS), BF16),
        in_specs=[anywhere] * 5,
        out_specs=anywhere,
        scratch_shapes=[
            pltpu.VMEM((UNITS, BANDS, 16, WIDE), BF16),
            pltpu.SMEM(pair_mask.shape, jnp.int32),
            *[pltpu.VMEM(value.shape, value.dtype) for value in selects],
            pltpu.VMEM((OWN, STA, LAGS), BF16),
            pltpu.VMEM((UNITS, PER_UNIT, OWN, STA, LAGS), BF16),
            dma((4 + UNITS,)),
            dma((UNITS + 1,)),
        ],
        compiler_params=pltpu.CompilerParams(vmem_limit_bytes=60 * 1024 * 1024),
        cost_estimate=pl.CostEstimate(flops=1_000_000_000, bytes_accessed=4_000_000, transcendentals=0),
        name="assemble",
    )(held, own, pair_mask, *[jnp.asarray(value) for value in selects])
    return out[None]


def solution(mesh):
    return jax.shard_map(
        local,
        mesh=mesh,
        in_specs=(P(None, "sta", "freq"), P()),
        out_specs=P("sta", None, "freq", None, None),
        check_vma=False,
    )
```

```python
import functools
import math

import jax
import jax.numpy as jnp
import ml_dtypes
import numpy as np
from jax import lax
from jax.experimental import pallas as pl
from jax.experimental.pallas import tpu as pltpu
from jax.sharding import PartitionSpec as P

FREQS = 4096
LAGS = 512
HALF = LAGS // 2
STA = 24
BAND = 512
BANDS = 8
OWN = 3
UNITS = 4
PER_UNIT = 4
PAIRS = PER_UNIT * OWN
ROWS = PAIRS * STA
MAIN = 32
LEFT = 4
WIDE = 2 * LAGS + 128
INPUTS = 6
PARTS = 4
PACKED = 12 * BANDS
MESH = pl.DeviceIdType.MESH
F32 = jnp.float32
BF16 = jnp.bfloat16


def half_tables():
    bins = np.arange(FREQS, dtype=np.float64)[:, None]
    lags = np.arange(HALF, dtype=np.float64)[None, :] + 0.5
    angle = math.pi * bins * lags / FREQS
    both = np.concatenate([np.cos(angle), np.sin(angle)], axis=1) / math.sqrt(FREQS)
    return both.astype(np.float32).astype(ml_dtypes.bfloat16).reshape(BANDS, BAND, LAGS)


def padded(value):
    return np.pad(value, [(0, 0)] * (value.ndim - 2) + [(0, 8), (0, 0)])


def phases():
    angle = math.pi * np.arange(FREQS, dtype=np.float64) / (2 * FREQS)
    both = np.stack([np.cos(angle), np.sin(angle)])
    return both.reshape(2 * BANDS, 1, BAND).astype(np.float32)


def piece_select():
    select = np.zeros((4, BANDS * 16, STA), np.float32)
    for dest in range(BANDS):
        for jj in range(OWN):
            for part in range(2):
                for half in range(2):
                    row = dest * 16 + (jj * 2 + part) * 2 + half
                    select[part * 2 + half, row, OWN * dest + jj] = 1
    return select.astype(ml_dtypes.bfloat16)


def send_select():
    select = np.zeros((BANDS * (MAIN + 16), ROWS), np.float32)
    for dest in range(BANDS):
        for kk in range(PER_UNIT):
            for il in range(OWN):
                for jj in range(OWN):
                    r = kk * 9 + il * OWN + jj
                    column = (kk * OWN + jj) * STA + OWN * dest + il
                    if r < MAIN:
                        select[dest * MAIN + r, column] = 1
                    else:
                        for tile in range(4):
                            select[BANDS * MAIN + dest * 16 + tile * LEFT + r - MAIN, column] = 1
    return select.astype(ml_dtypes.bfloat16)


def final_select():
    main = np.zeros((ROWS, BANDS * MAIN), np.float32)
    left = np.zeros((4 * 72, BANDS * 16), np.float32)
    for source in range(BANDS):
        for kk in range(PER_UNIT):
            for il in range(OWN):
                for jj in range(OWN):
                    r = kk * 9 + il * OWN + jj
                    row = il * STA + OWN * source + jj
                    if r < MAIN:
                        main[kk * 72 + row, r // 16 * 128 + source * 16 + r % 16] = 1
                    else:
                        for tile in range(4):
                            left[tile * 72 + row, source * 16 + tile * LEFT + r - MAIN] = 1
    return main.astype(ml_dtypes.bfloat16), left.astype(ml_dtypes.bfloat16)


def flip():
    return np.eye(HALF, dtype=np.float32)[::-1].astype(ml_dtypes.bfloat16)


def dot(a, b):
    return jnp.dot(a, b, preferred_element_type=F32)


def kernel(
    *refs,
):
    inputs, m_out, own_out, refs = refs[:INPUTS], refs[INPUTS], refs[INPUTS + 1], refs[INPUTS + 2 :]
    held, refs = refs[:INPUTS], refs[INPUTS:]
    x_ref, piece_ref, phase_ref, table, send_ref, flip_ref = held
    (
    pieces, p_land, b_land, a_land, a_spec, b_spec, lre0, lim0, lre1, lim1, acc, prod, s_main, own,
    in_sem, b_send, b_recv, a_send, a_recv, ring_send, ring_recv, sib_send, sib_recv, o_send, o_recv, m_sem, own_sem,
    ) = refs
    sta, freq = lax.axis_index("sta"), lax.axis_index("freq")
    z, quad = sta // 4, sta % 4
    ylo, core = quad // 2, quad % 2
    xx, yhi = freq // 2, freq % 2

    fetches = [pltpu.make_async_copy(inputs[n], held[n], in_sem.at[n]) for n in range(INPUTS)]
    for fetch in fetches[:2]:
        fetch.start()

    def peer(dx, dh, dl, dz=0):
        return (
            (z + 8 - dz) % 8 * 4 + (ylo + dl) % 2 * 2 + core,
            (xx + dx) % 4 * 2 + (yhi + dh) % 2,
        )

    plane = [(dx, dh, dl) for dl in range(2) for dh in range(2) for dx in range(4)]
    plane.sort(key=lambda d: -(min(d[0], 4 - d[0]) + 2 * d[1] + d[2]))
    others = plane[:-1]
    group = [d for d in others if d[2] == 0]
    below = ((sta + 28) % 32, freq)
    nearby = [(*d, 1) for d in plane] + [(*d, 0) for d in others]
    sibling = (z * 4 + ylo * 2 + (1 - core), freq)

    barrier = pltpu.get_barrier_semaphore()
    for device in [peer(dx, dh, dl, -dz) for dx, dh, dl, dz in nearby] + [sibling]:
        pl.semaphore_signal(barrier, inc=1, device_id=device, device_id_type=MESH)

    for fetch in fetches[2:]:
        fetch.start()
    fetches[0].wait()
    fetches[1].wait()
    total = None
    for part in range(2):
        for half in range(2):
            term = dot(piece_ref[part * 2 + half, :128], x_ref[part, :, half * 256 : half * 256 + 256])
            total = term if total is None else total + term
    pieces[...] = total.astype(BF16).reshape(BANDS, 16, 256)

    pl.semaphore_wait(barrier, len(nearby) + 1)

    def remote(src, dst, send, recv, device):
        return pltpu.make_async_remote_copy(
            src_ref=src, dst_ref=dst, send_sem=send, recv_sem=recv, device_id=device, device_id_type=MESH
        )

    b_copies = []
    for n, d in enumerate(nearby):
        device = peer(*d)
        b_copies.append(
            remote(pieces.at[device[1]], p_land.at[d[3], ylo, freq], b_send.at[n], b_recv.at[n], device)
        )
    a_copies = []
    for n, d in enumerate(group):
        a_copies.append(remote(x_ref, a_land.at[freq], a_send.at[n], a_recv.at[n], peer(*d)))
    for copy in b_copies + a_copies:
        copy.start()
    p_land[0, ylo, freq] = pieces[freq]
    a_land[freq] = x_ref[...]

    def ring(s, part):
        y, h = part // 2, pl.ds(part % 2 * 48, 48)
        return remote(
            b_land.at[s, core, y, h], b_land.at[s + 1, core, y, h], ring_send.at[s, part], ring_recv.at[s, part], below
        )

    def across(s, part):
        y, h = part // 2, pl.ds(part % 2 * 48, 48)
        return remote(
            b_land.at[s, core, y, h], b_land.at[s, core, y, h], sib_send.at[s, part], sib_recv.at[s, part], sibling
        )

    def forward(s):
        for part in range(PARTS):
            if s > 1:
                ring(s - 1, part).wait_recv()
            if 0 < s < UNITS:
                ring(s, part).start()
            across(s, part).start()

    row = lax.broadcasted_iota(jnp.int32, (PACKED, BANDS * 16), 0)
    column = lax.broadcasted_iota(jnp.int32, (PACKED, BANDS * 16), 1)
    pack = jnp.where(column == row % BANDS * 16 + row // BANDS, 1.0, 0.0).astype(BF16)
    for s in (1, 0):
        for d, copy in zip(nearby, b_copies):
            if d[3] == s:
                copy.wait_recv()
        for y in range(2):
            b_land[s, core, y] = dot(pack, p_land[s, y].reshape(BANDS * 16, 256)).astype(BF16)
        forward(s)

    for copy in a_copies:
        copy.wait_recv()

    def rotate(h, carry):
        cos, sin = phase_ref[h], phase_ref[BANDS + h]
        re = a_land[h, 0].astype(F32)
        im = a_land[h, 1].astype(F32)
        a_spec[h, 0] = re * cos + im * sin
        a_spec[h, 1] = im * cos - re * sin
        return carry

    fetches[2].wait()
    lax.fori_loop(0, BANDS, rotate, 0)
    for fetch in fetches[3:]:
        fetch.wait()

    def products(cross, rows):
        buffers = ((lre0, lim0), (lre1, lim1))

        def fill(two):
            for e in range(2):
                cross(2 * two + e, buffers[two % 2], e * BAND)

        def project(two):
            for n, part in enumerate(buffers[two % 2]):
                columns = slice(n * HALF, n * HALF + HALF)
                basis = table[2 * two : 2 * two + 2, :BAND, columns].reshape(2 * BAND, HALF)
                term = dot(part[:rows], basis)
                acc[:rows, columns] = term if two == 0 else acc[:rows, columns] + term

        fill(0)
        for two in range(BANDS // 2):
            if two + 1 < BANDS // 2:
                fill(two + 1)
            project(two)
        cos, sin = acc[:rows, :HALF], acc[:rows, HALF:]
        return (cos + sin).astype(BF16), (cos - sin).astype(BF16)

    def cross_unit(h, buffers, start):
        for half in range(2):
            lanes = slice(half * 256, half * 256 + 256)
            place = slice(start + half * 256, start + half * 256 + 256)
            ar, ai = a_spec[h, 0, :, lanes], a_spec[h, 1, :, lanes]
            for two in range(PAIRS // 2):
                re, im = [], []
                for g in (2 * two, 2 * two + 1):
                    kk, jj = g // OWN, g % OWN
                    row = jj * 4 + half
                    br = b_spec[kk, row, h : h + 1, :]
                    bi = b_spec[kk, row + 2, h : h + 1, :]
                    re.append(ar * br + ai * bi)
                    im.append(ai * br - ar * bi)
                buffers[0][two * 48 : two * 48 + 48, place] = jnp.concatenate(re, axis=0).astype(BF16)
                buffers[1][two * 48 : two * 48 + 48, place] = jnp.concatenate(im, axis=0).astype(BF16)

    def cross_own(h, buffers, start):
        for half in range(2):
            lanes = slice(half * 256, half * 256 + 256)
            place = slice(start + half * 256, start + half * 256 + 256)
            br = a_land[h, 0, :, lanes].astype(F32)
            bi = a_land[h, 1, :, lanes].astype(F32)
            re, im = [], []
            for il in (0, 1, 2, 2):
                ar = a_spec[h, 0, pl.ds(OWN * freq + il, 1), lanes]
                ai = a_spec[h, 1, pl.ds(OWN * freq + il, 1), lanes]
                re.append(ar * br + ai * bi)
                im.append(ai * br - ar * bi)
            buffers[0][:96, place] = jnp.concatenate(re, axis=0).astype(BF16)
            buffers[1][:96, place] = jnp.concatenate(im, axis=0).astype(BF16)

    def out_copies(unit):
        copies = []
        for n, d in enumerate(group):
            device = peer(*d)
            copies.append(
                remote(s_main.at[unit, device[1]], m_out.at[unit, freq], o_send.at[unit, n], o_recv.at[unit, n], device)
            )
        return copies

    def kept(unit):
        return pltpu.make_async_copy(s_main.at[unit, freq], m_out.at[unit, freq], m_sem.at[unit])

    tile = lax.broadcasted_iota(jnp.int32, (BANDS * 16, 128), 0) // LEFT % 4

    for unit in range(UNITS):
        if unit + 2 <= UNITS:
            forward(unit + 2)
        for s in ([0, 1] if unit == 0 else [unit + 1]):
            for part in range(PARTS):
                across(s, part).wait_recv()
        for kk in range(PER_UNIT):
            slot = quad + unit * PER_UNIT + 1 + kk
            spot = slot % 4
            b_spec[kk] = b_land[slot // 4, spot % 2, spot // 2].astype(F32).reshape(12, BANDS, 256)
        low, high = products(cross_unit, ROWS)
        prod[:, :HALF] = dot(low, flip_ref[:HALF]).astype(BF16)
        prod[:, HALF:] = high
        rows = dot(send_ref[: BANDS * (MAIN + 16)], prod[...])
        main = rows[: BANDS * MAIN].astype(BF16).reshape(BANDS, 2, 16, LAGS)
        s_main[unit, :, :, :LAGS] = main[:, 0]
        s_main[unit, :, :, LAGS : 2 * LAGS] = main[:, 1]
        rows = rows[BANDS * MAIN :]
        left = rows[:, :128]
        for t in range(1, 4):
            left = jnp.where(tile == t, rows[:, t * 128 : t * 128 + 128], left)
        s_main[unit, :, :, 2 * LAGS :] = left.astype(BF16).reshape(BANDS, 16, 128)
        for copy in out_copies(unit):
            copy.start()
        kept(unit).start()

    low, high = products(cross_own, 96)
    low = dot(low, flip_ref[:HALF])
    value = jnp.concatenate([low, high.astype(F32)], axis=1)[:72]
    row = lax.broadcasted_iota(jnp.int32, (72, LAGS), 0)
    mine = row // STA + OWN * freq
    own[...] = jnp.where(row % STA != mine, value, 0.0).reshape(OWN, STA, LAGS).astype(BF16)
    own_copy = pltpu.make_async_copy(own, own_out, own_sem)
    own_copy.start()

    for unit in range(UNITS):
        for copy in out_copies(unit):
            copy.wait_recv()
        kept(unit).wait()
    own_copy.wait()
    for copy in b_copies + a_copies:
        copy.wait_send()
    for unit in range(UNITS):
        for copy in out_copies(unit):
            copy.wait_send()
        if unit > 0:
            for part in range(PARTS):
                ring(unit, part).wait_send()
    for s in range(UNITS + 1):
        for part in range(PARTS):
            across(s, part).wait_send()


def assemble(m_hbm, own_hbm, mask_hbm, main_hbm, left_hbm, out_hbm, m, mask, main_ref, left_ref, own, done, in_sem, out_sem):
    sta = lax.axis_index("sta")
    sources = [main_hbm, left_hbm, mask_hbm, own_hbm] + [m_hbm.at[unit] for unit in range(UNITS)]
    targets = [main_ref, left_ref, mask, own] + [m.at[unit] for unit in range(UNITS)]
    fetches = [pltpu.make_async_copy(a, b, in_sem.at[n]) for n, (a, b) in enumerate(zip(sources, targets))]
    for fetch in fetches:
        fetch.start()
    for fetch in fetches[:4]:
        fetch.wait()
    stores = [pltpu.make_async_copy(own, out_hbm.at[0], out_sem.at[UNITS])]
    stores[0].start()
    for pair in ((0, 1), (2, 3)):
        for unit in pair:
            fetches[4 + unit].wait()
        for unit in pair:
            halves = [m[unit, :, :, half * LAGS : half * LAGS + LAGS].reshape(BANDS * 16, LAGS) for half in range(2)]
            rows = dot(main_ref[:ROWS], jnp.concatenate(halves, axis=0))
            left = dot(left_ref[: 4 * 72], m[unit, :, :, 2 * LAGS :].reshape(BANDS * 16, 128))
            left = jnp.concatenate([left[t * 72 : t * 72 + 72] for t in range(4)], axis=1)
            for kk in range(PER_UNIT):
                value = rows[kk * 72 : kk * 72 + 72]
                if kk == PER_UNIT - 1:
                    value = value + left
                on = mask[sta, (sta + unit * PER_UNIT + 1 + kk) % 32] > 0
                done[unit, kk] = jnp.where(on, value, 0.0).reshape(OWN, STA, LAGS).astype(BF16)
        for unit in pair:
            store = pltpu.make_async_copy(done.at[unit], out_hbm.at[pl.ds(1 + unit * PER_UNIT, PER_UNIT)], out_sem.at[unit])
            store.start()
            stores.append(store)
    for store in stores:
        store.wait()


def local(spectra, pair_mask):
    main, left = final_select()
    arrays = [spectra, padded(piece_select()), phases(), padded(half_tables()), padded(send_select()), padded(flip())]
    dma = pltpu.SemaphoreType.DMA
    anywhere = pl.BlockSpec(memory_space=pl.ANY)
    held, own = pl.pallas_call(
        kernel,
        out_shape=[
            jax.ShapeDtypeStruct((UNITS, BANDS, 16, WIDE), BF16),
            jax.ShapeDtypeStruct((OWN, STA, LAGS), BF16),
        ],
        in_specs=[anywhere] * INPUTS,
        out_specs=[anywhere] * 2,
        scratch_shapes=[
            *[pltpu.VMEM(value.shape, value.dtype) for value in arrays],
            pltpu.VMEM((BANDS, 16, 256), BF16),
            pltpu.VMEM((2, 2, BANDS, 16, 256), BF16),
            pltpu.VMEM((UNITS + 1, 2, 2, PACKED, 256), BF16),
            pltpu.VMEM((BANDS, 2, STA, BAND), BF16),
            pltpu.VMEM((BANDS, 2, STA, BAND), F32),
            pltpu.VMEM((PER_UNIT, 12, BANDS, 256), F32),
            pltpu.VMEM((ROWS, 2 * BAND), BF16),
            pltpu.VMEM((ROWS, 2 * BAND), BF16),
            pltpu.VMEM((ROWS, 2 * BAND), BF16),
            pltpu.VMEM((ROWS, 2 * BAND), BF16),
            pltpu.VMEM((ROWS, LAGS), F32),
            pltpu.VMEM((ROWS, LAGS), BF16),
            pltpu.VMEM((UNITS, BANDS, 16, WIDE), BF16),
            pltpu.VMEM((OWN, STA, LAGS), BF16),
            dma((INPUTS,)),
            dma((31,)),
            dma((31,)),
            dma((7,)),
            dma((7,)),
            dma((UNITS, PARTS)),
            dma((UNITS, PARTS)),
            dma((UNITS + 1, PARTS)),
            dma((UNITS + 1, PARTS)),
            dma((UNITS, 7)),
            dma((UNITS, 7)),
            dma((UNITS,)),
            dma,
        ],
        compiler_params=pltpu.CompilerParams(
            collective_id=0, has_side_effects=True, vmem_limit_bytes=60 * 1024 * 1024
        ),
        cost_estimate=pl.CostEstimate(flops=10_000_000_000, bytes_accessed=8_000_000, transcendentals=0),
        name="correlate",
    )(*[jnp.asarray(value) for value in arrays])
    selects = [padded(main), padded(left)]
    out = pl.pallas_call(
        assemble,
        out_shape=jax.ShapeDtypeStruct((17, OWN, STA, LAGS), BF16),
        in_specs=[anywhere] * 5,
        out_specs=anywhere,
        scratch_shapes=[
            pltpu.VMEM((UNITS, BANDS, 16, WIDE), BF16),
            pltpu.SMEM(pair_mask.shape, jnp.int32),
            *[pltpu.VMEM(value.shape, value.dtype) for value in selects],
            pltpu.VMEM((OWN, STA, LAGS), BF16),
            pltpu.VMEM((UNITS, PER_UNIT, OWN, STA, LAGS), BF16),
            dma((4 + UNITS,)),
            dma((UNITS + 1,)),
        ],
        compiler_params=pltpu.CompilerParams(vmem_limit_bytes=60 * 1024 * 1024),
        cost_estimate=pl.CostEstimate(flops=1_000_000_000, bytes_accessed=4_000_000, transcendentals=0),
        name="assemble",
    )(held, own, pair_mask, *[jnp.asarray(value) for value in selects])
    return out[None]


def solution(mesh):
    return jax.shard_map(
        local,
        mesh=mesh,
        in_specs=(P(None, "sta", "freq"), P()),
        out_specs=P("sta", None, "freq", None, None),
        check_vma=False,
    )
```
